128 devices in a mesh: ctx: 32 (over y, x, core), head: 4 (over z).
Axes of the slice: x: 4, y: 4, z: 4, core: 2. Of those that a mesh axis runs over, the one named last changes fastest.
Arguments:
- queries: bfloat16 [4096, 1024], P('ctx', 'head'), may hold values from -6 to 6
- grad_out: bfloat16 [4096, 1024], P('ctx', 'head'), may hold values from -384 to 384
- saved_out: bfloat16 [4096, 1024], P('ctx', 'head'), may hold values from -0.59765625 to 0.59765625
- saved_lse: float32 [8, 4096], P('head', 'ctx'), may hold values from 9.5 to 11.5
- prefix_keys: bfloat16 [65536, 128], P('ctx'), may hold values from -6 to 6
- prefix_values: bfloat16 [65536, 128], P('ctx'), may hold values from -6 to 6
- span_keys: bfloat16 [4096, 128], P('ctx'), may hold values from -6 to 6
- span_values: bfloat16 [4096, 128], P('ctx'), may hold values from -6 to 6
- positions: int32 [4096], replicated, may hold values from 0 to 4095, each once
- prefix_len: int32 [32], P('ctx'), may hold values from 1 to 2048, 32768 in all
Outputs:
- query_grad: float32 [4096, 1024], P('ctx', 'head')
- prefix_key_grad: float32 [65536, 128], P(('ctx', 'head'))
- prefix_value_grad: float32 [65536, 128], P(('ctx', 'head'))
- span_key_grad: float32 [4096, 128], P(('ctx', 'head'))
- span_value_grad: float32 [4096, 128], P(('ctx', 'head'))
The draws below stay inside these ranges and needn't reach their ends.
Inputs may be any that keep to these rules, and one draw needn't show every extreme that they name: `positions`: each of 0 to 4095 appears once. `prefix_len`: the first that many rows of each shard's block of 2048 prefix rows are valid; some shard is full.
All inputs are finite; a program needn't handle non-finite values.
Results may differ from the reference program's by a relative error of at most 0.015.
Values may be sent and summed in bfloat16 or wider, within the bound.
No kernel may reach another device: no remote copies, remote signals or barrier semaphores. Data moves between devices by JAX's collectives and lax.ppermute only.
A program may use at most 64 MiB of HBM per device.

```python
import math
import jax
import jax.numpy as jnp
import numpy as np
from jax import lax

HEADS = 8
HD = 128
Q_DEV = 128
P_DEV = 2048
SPAN = 4096
PREFIX = 65536
N_CTX = 32
N_HEAD = 4


def block_scale(key, dims, pieces, low, largest):
    factor_of = 1.0
    for dim, shards_of in pieces:
        draws = jax.random.uniform(jax.random.fold_in(jax.random.fold_in(key, 6), dim), (shards_of,), jnp.float32, low / len(pieces), largest / len(pieces))
        factor_of = factor_of * jnp.repeat(jnp.exp(draws), dims[dim] // shards_of).reshape((-1,) + (1,) * (len(dims) - 1 - dim))
    return factor_of


def length_profile(amount, total, limit, skew):
    portions = [(1 << 20) // math.isqrt(standing ** skew) + 1 for standing in range(2, amount + 1)]
    spare, counts = total - limit - (amount - 1), [1] * (amount - 1)
    while spare > 0:
        movable = [i for i in range(amount - 1) if counts[i] < limit]
        whole, remaining = sum([portions[i] for i in movable]), spare
        for i in movable:
            extra = min(limit - counts[i], max(1, remaining * portions[i] // whole), spare)
            counts[i] = counts[i] + extra
            spare = spare - extra
    return np.array([limit] + counts)


def uneven(own_key, amount, total, most, lean):
    if amount == 2:
        one = jax.random.randint(own_key, (), max(1, total - most), min(most, total - 1) + 1)
        return jnp.stack([one, total - one])
    tallies = jnp.asarray(length_profile(amount, total, most, lean), jnp.int32)
    couples = (amount - 1) // 2
    giver, receiver = tallies[1:1 + 2 * couples:2], tallies[2:2 + 2 * couples:2]
    room = jnp.minimum(giver - 1, most - receiver)
    shifted = jax.random.randint(jax.random.fold_in(own_key, 1), (couples,), 0, 1 << 20) % (room + 1)
    tallies = tallies.at[1:1 + 2 * couples:2].set(giver - shifted).at[2:2 + 2 * couples:2].set(receiver + shifted)
    return tallies[jax.random.permutation(jax.random.fold_in(own_key, 2), amount)]


def noise(key, shape, spread, limit, shards=(), held_as=jnp.bfloat16):
    array = jax.random.normal(key, shape, jnp.float32) * spread
    if len(shards) > 0:
        array = block_scale(key, shape, shards, -0.22, 0.18) * array
    return jnp.clip(array, min=-limit, max=limit).astype(held_as)


def setup_inputs(seed: int = 0) -> dict:
    streams_of = jax.random.split(jax.random.key(seed), 11)
    return {
        "queries": noise(streams_of[0], (SPAN, HEADS * HD), 1.0, 6.0, ((0, 32), (1, 4))),
        "grad_out": noise(streams_of[1], (SPAN, HEADS * HD), 64.0, 384.0, ((0, 32), (1, 4))),
        "saved_out": noise(streams_of[2], (SPAN, HEADS * HD), 0.1, 0.59765625, ((0, 32), (1, 4))),
        "saved_lse": jnp.clip(9.5 + 2.0 * jax.random.uniform(streams_of[3], (HEADS, SPAN), jnp.float32) ** block_scale(streams_of[3], (HEADS, SPAN), ((0, 4), (1, 32)), -0.2, 0.2), 9.5, 11.5),
        "prefix_keys": noise(streams_of[4], (PREFIX, HD), 1.0, 6.0, ((0, 32),)),
        "prefix_values": noise(streams_of[5], (PREFIX, HD), 1.0, 6.0, ((0, 32),)),
        "span_keys": noise(streams_of[6], (SPAN, HD), 1.0, 6.0, ((0, 32),)),
        "span_values": noise(streams_of[7], (SPAN, HD), 1.0, 6.0, ((0, 32),)),
        "positions": jax.random.permutation(streams_of[8], SPAN).astype(jnp.int32),
        "prefix_len": uneven(streams_of[9], N_CTX, N_CTX * P_DEV // 2, P_DEV, 0).astype(jnp.int32),
    }


def to_low(values):
    return lax.optimization_barrier(values.astype(jnp.bfloat16)).astype(jnp.float32)


def reference(queries, grad_out, saved_out, saved_lse, prefix_keys, prefix_values, span_keys, span_values, positions, prefix_len):
    factor = HD ** -0.5
    group_heads = HEADS // N_HEAD
    all_keys = jnp.concatenate([prefix_keys, span_keys], axis=0).astype(jnp.float32)
    all_values = jnp.concatenate([prefix_values, span_values], axis=0).astype(jnp.float32)
    prefix_split = prefix_keys.astype(jnp.float32).reshape(N_CTX, P_DEV, HD)
    span_split = span_keys.astype(jnp.float32).reshape(N_CTX, Q_DEV, HD)
    limits = jnp.repeat(prefix_len, P_DEV)
    prefix_ok = (jnp.arange(PREFIX, dtype=jnp.int32) % P_DEV) < limits
    grad_three = grad_out.astype(jnp.float32).reshape(SPAN, HEADS, HD)
    out_three = saved_out.astype(jnp.float32).reshape(SPAN, HEADS, HD)
    query_three = queries.astype(jnp.float32).reshape(SPAN, HEADS, HD)
    deltas = jnp.sum(grad_three * out_three, axis=2)
    block_rows = math.gcd(SPAN, 64)
    key_total = PREFIX + SPAN

    def visit_block(totals, first_row):
        query_block = lax.dynamic_slice_in_dim(query_three, first_row, block_rows, 0)
        grad_block = lax.dynamic_slice_in_dim(grad_three, first_row, block_rows, 0)
        lse_block = lax.dynamic_slice_in_dim(saved_lse, first_row, block_rows, 1)
        delta_block = lax.dynamic_slice_in_dim(deltas, first_row, block_rows, 0).T
        query_pos = lax.dynamic_slice_in_dim(positions, first_row, block_rows, 0)
        visible = jnp.concatenate([jnp.broadcast_to(prefix_ok[None, :], (block_rows, PREFIX)), positions[None, :] <= query_pos[:, None]], axis=1)
        logits = jnp.einsum('ihd,jd->hij', query_block, all_keys) * factor
        probs = jnp.where(visible[None], jnp.exp(logits - lse_block[:, :, None]), 0.0)
        dot_grad = jnp.einsum('ihd,jd->hij', grad_block, all_values)
        score_grad = probs * (dot_grad - delta_block[:, :, None])
        probs_low = to_low(probs)
        score_low = to_low(score_grad)
        score_groups = score_low.reshape(N_HEAD, group_heads, block_rows, key_total)
        probs_groups = probs_low.reshape(N_HEAD, group_heads, block_rows, key_total)
        query_groups = query_block.reshape(block_rows, N_HEAD, group_heads, HD)
        grad_groups = grad_block.reshape(block_rows, N_HEAD, group_heads, HD)
        key_grad = totals[0] + jnp.einsum('gkij,igkd->gjd', score_groups, query_groups)
        value_grad = totals[1] + jnp.einsum('gkij,igkd->gjd', probs_groups, grad_groups)
        score_prefix = score_low[:, :, :PREFIX].reshape(HEADS, block_rows, N_CTX, P_DEV)
        score_span = score_low[:, :, PREFIX:].reshape(HEADS, block_rows, N_CTX, Q_DEV)
        shard_parts = jnp.einsum('hicj,cjd->cihd', score_prefix, prefix_split) + jnp.einsum('hicj,cjd->cihd', score_span, span_split)
        dq_block = jnp.sum(to_low(shard_parts * factor), axis=0).reshape(block_rows, HEADS * HD)
        return (key_grad, value_grad), dq_block

    zeros_kv = jnp.zeros((N_HEAD, key_total, HD), jnp.float32)
    firsts = jnp.arange(0, SPAN, block_rows, dtype=jnp.int32)
    (key_parts, value_parts), dq_blocks = lax.scan(visit_block, (zeros_kv, zeros_kv), firsts)
    query_grad = dq_blocks.reshape(SPAN, HEADS * HD)
    key_grad = jnp.sum(to_low(key_parts * factor), axis=0)
    value_grad = jnp.sum(to_low(value_parts), axis=0)
    return (query_grad, key_grad[:PREFIX], value_grad[:PREFIX], key_grad[PREFIX:], value_grad[PREFIX:])
```

```python
import functools
import math

import jax
import jax.numpy as jnp
from jax import lax
from jax.experimental import pallas as pl
from jax.experimental.pallas import tpu as pltpu
from jax.sharding import PartitionSpec as P

BF16 = jnp.bfloat16
F32 = jnp.float32
AUX = 16
LOG2E = math.log2(math.e)


def contract(a, b, dim_a, dim_b):
    return lax.dot_general(a, b, (((dim_a,), (dim_b,)), ((), ())), preferred_element_type=F32)


def attention_kernel(sizes, first, last, *refs):
    groups, rows_src, prefix, span, block, row_block, head_dim, heads_z = sizes
    rows = groups * rows_src
    refs = list(refs)
    lens, x, kv_own, kv_par, pos_q, pos_k = refs[:6]
    refs = refs[6:]
    if not first:
        acc_k_in, acc_v_in = refs[:2]
        refs = refs[2:]
    dq_out, out_a, out_b = refs[:3]
    kc, vc, qs, ds_, ld, dq_t = refs[3:9]
    if last:
        acc_k, acc_v = refs[9:11]
    else:
        acc_k, acc_v = out_a, out_b
    half = block // 2
    scale = head_dim ** -0.5
    len_own, len_par = lens[0], lens[1]
    offset = pl.multiple_of(2 * span + ((len_own + 15) // 16) * 16, 16)

    for s in range(groups):
        here = pl.ds(s * rows_src, rows_src)
        qs[here, :] = x[s, AUX:, :head_dim]
        ds_[here, :] = x[s, AUX:, head_dim:]
        pieces = x[s, :AUX, :].astype(F32)
        total = pieces[0:1] + pieces[1:2] + pieces[2:3]
        ld[0:1, here] = total[:, :rows_src]
        ld[1:2, here] = total[:, head_dim:head_dim + rows_src]

    def masked(ref, columns, length):
        index = lax.broadcasted_iota(jnp.int32, (prefix, head_dim), 0)
        return jnp.where(index < length, ref[:prefix, columns], jnp.zeros((), BF16))

    for packed, columns in ((kc, slice(0, head_dim)), (vc, slice(head_dim, 2 * head_dim))):
        packed[0:span, :] = kv_own[prefix:prefix + span, columns]
        packed[span:2 * span, :] = kv_par[prefix:prefix + span, columns]
        packed[2 * span:2 * span + prefix, :] = masked(kv_own, columns, len_own)
        packed[pl.ds(offset, prefix), :] = masked(kv_par, columns, len_par)
        packed[pl.ds(pl.multiple_of(offset + prefix, 16), block), :] = jnp.zeros((block, head_dim), BF16)

    dq_t[...] = jnp.zeros_like(dq_t)
    if first:
        acc_k[...] = jnp.zeros_like(acc_k)
        acc_v[...] = jnp.zeros_like(acc_v)
    else:
        acc_k[...] = acc_k_in[...]
        acc_v[...] = acc_v_in[...]

    def step(start, width, causal):
        here = pl.ds(start, width)
        keys, values = kc[here, :], vc[here, :]
        for i in range(rows // row_block):
            some = pl.ds(i * row_block, row_block)
            queries, grads = qs[some, :], ds_[some, :]
            logits = contract(keys, queries, 1, 1)
            probs = jnp.exp2(logits * (scale * LOG2E) - ld[0:1, some])
            if causal:
                probs = jnp.where(pos_k[...] <= pos_q[0:1, some], probs, 0.0)
            dot_grad = contract(values, grads, 1, 1)
            score_low = (probs * (dot_grad - ld[1:2, some])).astype(BF16)
            probs_low = probs.astype(BF16)
            acc_v[here, :] += contract(probs_low, grads, 1, 0)
            acc_k[here, :] += contract(score_low, queries, 1, 0)
            dq_t[:, some] += contract(keys, score_low, 0, 0)

    step(0, 2 * span, True)
    halves = (offset - 2 * span + len_par + half - 1) // half
    wholes = halves // 2

    def whole(i, carry):
        step(pl.multiple_of(2 * span + i * block, half), block, False)
        return carry

    lax.fori_loop(0, wholes, whole, 0)

    @pl.when(halves % 2 == 1)
    def _():
        step(pl.multiple_of(2 * span + wholes * block, half), half, False)

    for s in range(groups):
        here = pl.ds(s * rows_src, rows_src)
        dq_out[here, :] = (dq_t[:, here] * scale).T.astype(BF16)

    if last:
        part, part_span = prefix // heads_z, span // heads_z
        for out, begin, length, span_at in ((out_a, 2 * span, len_own, 0), (out_b, offset, len_par, span)):
            for z in range(heads_z):
                for acc, columns, factor in (
                    (acc_k, slice(0, head_dim), scale),
                    (acc_v, slice(head_dim, 2 * head_dim), 1.0),
                ):
                    index = lax.broadcasted_iota(jnp.int32, (part, head_dim), 0) + z * part
                    at = pl.multiple_of(begin + z * part, 16)
                    valid = jnp.where(index < length, acc[pl.ds(at, part), :] * factor, 0.0)
                    out[z, :part, columns] = valid.astype(BF16)
                    out[z, part:, columns] = (
                        acc[pl.ds(span_at + z * part_span, part_span), :] * factor
                    ).astype(BF16)


def attend(first, last, heads_z, lens, x, kv_own, kv_par, pos_q, pos_k, carried):
    groups, rows_src, head_dim = x.shape[0], x.shape[1] - AUX, x.shape[2] // 2
    rows = groups * rows_src
    span = pos_k.shape[0] // 2
    prefix = kv_own.shape[0] - span
    block, row_block = 512, min(rows, 2048)
    packed_rows = 2 * span + 2 * prefix + block
    sizes = (groups, rows_src, prefix, span, block, row_block, head_dim, heads_z)
    vmem = pl.BlockSpec(memory_space=pltpu.VMEM)
    acc_type = jax.ShapeDtypeStruct((packed_rows, head_dim), F32)
    part_type = jax.ShapeDtypeStruct((heads_z, (prefix + span) // heads_z, 2 * head_dim), BF16)
    scratch = [
        pltpu.VMEM((packed_rows, head_dim), BF16),
        pltpu.VMEM((packed_rows, head_dim), BF16),
        pltpu.VMEM((rows, head_dim), BF16),
        pltpu.VMEM((rows, head_dim), BF16),
        pltpu.VMEM((2, rows), F32),
        pltpu.VMEM((head_dim, rows), F32),
    ]
    if last:
        scratch += [pltpu.VMEM((packed_rows, head_dim), F32)] * 2
    return pl.pallas_call(
        functools.partial(attention_kernel, sizes, first, last),
        out_shape=(jax.ShapeDtypeStruct((rows, head_dim), BF16),) + ((part_type,) * 2 if last else (acc_type,) * 2),
        in_specs=[pl.BlockSpec(memory_space=pltpu.SMEM)] + [vmem] * (5 + len(carried)),
        out_specs=(vmem,) * 3,
        scratch_shapes=scratch,
        compiler_params=pltpu.CompilerParams(vmem_limit_bytes=58 * 2**20),
        cost_estimate=pl.CostEstimate(
            flops=10 * rows * head_dim * (prefix + 2 * span), bytes_accessed=8 * 2**20, transcendentals=0
        ),
    )(lens, x, kv_own, kv_par, pos_q, pos_k, *carried)


def split3(value):
    high = lax.reduce_precision(value, 8, 7)
    middle = lax.reduce_precision(value - high, 8, 7)
    low = value - high - middle
    return high.astype(BF16), middle.astype(BF16), low.astype(BF16)


def shards(
    n_ctx,
    n_head,
    queries,
    grad_out,
    saved_out,
    saved_lse,
    prefix_keys,
    prefix_values,
    span_keys,
    span_values,
    positions,
    prefix_len,
):
    heads_local = saved_lse.shape[0]
    rows_local = queries.shape[0]
    head_dim = queries.shape[1] // heads_local
    prefix_rows = prefix_keys.shape[0]
    chips = n_ctx // 2
    me = lax.axis_index("ctx")
    core = lax.rem(me, 2)
    chip = me // 2
    same_core = [[2 * i + c for i in range(chips)] for c in range(2)]
    swap = [(i, i ^ 1) for i in range(n_ctx)]

    kv_own = jnp.concatenate(
        [jnp.concatenate([prefix_keys, span_keys], 0), jnp.concatenate([prefix_values, span_values], 0)], 1
    )
    kv_par = lax.ppermute(kv_own, "ctx", swap)
    lens = jnp.concatenate([prefix_len, lax.ppermute(prefix_len, "ctx", swap)])

    deltas = jnp.einsum(
        "ihd,ihd->hi",
        grad_out.reshape(rows_local, heads_local, head_dim),
        saved_out.reshape(rows_local, heads_local, head_dim),
        preferred_element_type=F32,
    )
    aux = jnp.stack(split3(jnp.concatenate([saved_lse * LOG2E, deltas], 1)))
    aux = jnp.pad(aux, ((0, AUX - 3), (0, 0), (0, 0)))

    by_core = positions.reshape(chips, 2, rows_local)
    pos_q = lax.dynamic_index_in_dim(by_core, core, 1, False).reshape(1, chips * rows_local)
    pos_chip = lax.dynamic_index_in_dim(by_core, chip, 0, False)
    pos_k = jnp.where(core == 0, pos_chip, pos_chip[::-1]).reshape(2 * rows_local, 1)

    gathered = []
    for h in range(heads_local):
        columns = slice(h * head_dim, (h + 1) * head_dim)
        packed = jnp.concatenate(
            [aux[:, h], jnp.concatenate([queries[:, columns], grad_out[:, columns]], 1)], 0
        )
        sent = jnp.broadcast_to(packed[None], (chips,) + packed.shape)
        gathered.append(lax.all_to_all(sent, "ctx", 0, 0, axis_index_groups=same_core, tiled=True))

    carried = ()
    query_parts = []
    for h in range(heads_local):
        dq, *carried = attend(
            h == 0, h == heads_local - 1, n_head, lens, gathered[h], kv_own, kv_par, pos_q, pos_k, carried
        )
        arrived = lax.all_to_all(dq, "ctx", 0, 0, axis_index_groups=same_core, tiled=True)
        query_parts.append(arrived.reshape(chips, rows_local, head_dim).astype(F32).sum(0))
    query_grad = jnp.concatenate(query_parts, 1)

    own, other = carried
    both = own.astype(F32) + lax.ppermute(other, "ctx", swap).astype(F32)
    parts = lax.all_to_all(both.astype(BF16), "head", 0, 0, tiled=True).astype(F32).sum(0)
    part = prefix_rows // n_head
    return (
        query_grad,
        parts[:part, :head_dim],
        parts[:part, head_dim:],
        parts[part:, :head_dim],
        parts[part:, head_dim:],
    )


def solution(mesh):
    in_specs = (
        P("ctx", "head"),
        P("ctx", "head"),
        P("ctx", "head"),
        P("head", "ctx"),
        P("ctx", None),
        P("ctx", None),
        P("ctx", None),
        P("ctx", None),
        P(),
        P("ctx"),
    )
    out_specs = (
        P("ctx", "head"),
        P(("ctx", "head"), None),
        P(("ctx", "head"), None),
        P(("ctx", "head"), None),
        P(("ctx", "head"), None),
    )
    body = functools.partial(shards, mesh.shape["ctx"], mesh.shape["head"])
    return jax.shard_map(body, mesh=mesh, in_specs=in_specs, out_specs=out_specs, check_vma=False)
```

```python
import functools
import math

import jax
import jax.numpy as jnp
from jax import lax
from jax.experimental import pallas as pl
from jax.experimental.pallas import tpu as pltpu
from jax.sharding import PartitionSpec as P

BF16 = jnp.bfloat16
F32 = jnp.float32
AUX = 16
LOG2E = math.log2(math.e)
BLOCK = 512
ROW_BLOCK = 2048
VMEM_MIB = 52


def contract(a, b, dim_a, dim_b):
    return lax.dot_general(a, b, (((dim_a,), (dim_b,)), ((), ())), preferred_element_type=F32)


def load_rows(x, queries, grads, lse_delta):
    groups, rows_src, head_dim = x.shape[0], x.shape[1] - AUX, x.shape[2] // 2
    for s in range(groups):
        here = pl.ds(s * rows_src, rows_src)
        queries[here, :] = x[s, AUX:, :head_dim]
        grads[here, :] = x[s, AUX:, head_dim:]
        pieces = x[s, :AUX, :].astype(F32)
        total = pieces[0:1] + pieces[1:2] + pieces[2:3]
        lse_delta[0:1, here] = total[:, :rows_src]
        lse_delta[1:2, here] = total[:, head_dim:head_dim + rows_src]


def visit_shard(prefix, length, kv, pos_k, pos_q, queries, grads, lse_delta, dq_t, add):
    rows, head_dim = queries.shape
    span = kv.shape[0] - prefix
    row_block = min(rows, ROW_BLOCK)
    scale = head_dim ** -0.5

    def step(start, width, causal, masked):
        here = pl.ds(start, width)
        keys, values = kv[here, :head_dim], kv[here, head_dim:]
        if masked:
            index = lax.broadcasted_iota(jnp.int32, (width, head_dim), 0) + start
            keys = jnp.where(index < length, keys, jnp.zeros((), BF16))
            values = jnp.where(index < length, values, jnp.zeros((), BF16))
        key_grad, value_grad = 0.0, 0.0
        for i in range(rows // row_block):
            some = pl.ds(i * row_block, row_block)
            query, grad = queries[some, :], grads[some, :]
            logits = contract(keys, query, 1, 1)
            probs = jnp.exp2(logits * (scale * LOG2E) - lse_delta[0:1, some])
            if causal:
                probs = jnp.where(pos_k <= pos_q[0:1, some], probs, 0.0)
            dot_grad = contract(values, grad, 1, 1)
            score_low = (probs * (dot_grad - lse_delta[1:2, some])).astype(BF16)
            value_grad += contract(probs.astype(BF16), grad, 1, 0)
            key_grad += contract(score_low, query, 1, 0)
            dq_t[:, some] += contract(keys, score_low, 0, 0)
        add(start, width, masked, key_grad, value_grad)

    quarter = BLOCK // 4
    step(prefix, span, True, False)
    pieces = (length + quarter - 1) // quarter
    wholes = length // BLOCK

    def whole(i, carry):
        step(pl.multiple_of(i * BLOCK, BLOCK), BLOCK, False, False)
        return carry

    lax.fori_loop(0, wholes, whole, 0)
    left = pieces - 4 * wholes

    @pl.when(left == 4)
    def _():
        step(pl.multiple_of(wholes * BLOCK, BLOCK), BLOCK, False, True)

    @pl.when((left == 2) | (left == 3))
    def _():
        step(pl.multiple_of(wholes * BLOCK, BLOCK), 2 * quarter, False, True)

    @pl.when((left == 1) | (left == 3))
    def _():
        step(pl.multiple_of((pieces - 1) * quarter, quarter), quarter, False, True)


def store_query_grad(dq_t, out, rows_src):
    scale = dq_t.shape[0] ** -0.5
    for s in range(dq_t.shape[1] // rows_src):
        here = pl.ds(s * rows_src, rows_src)
        out[here, :] = (dq_t[:, here] * scale).T.astype(BF16)


def collect(prefix, length, before, out):
    heads_z, _, columns = out.shape
    part, part_span = prefix // heads_z, out.shape[1] - prefix // heads_z
    scale = (columns // 2) ** -0.5
    out[...] = jnp.zeros_like(out)

    def add(start, width, masked, key_grad, value_grad):
        both = jnp.concatenate([key_grad * scale, value_grad], 1)
        if isinstance(start, int):
            for z in range(heads_z):
                rows = both[z * part_span:(z + 1) * part_span]
                if before is not None:
                    rows += before[z, part:, :].astype(F32)
                out[z, part:, :] = rows.astype(out.dtype)
            return
        z, here = start // part, pl.ds(pl.multiple_of(lax.rem(start, part), BLOCK // 4), width)
        if before is not None:
            both += before[z, here, :].astype(F32)
        if masked:
            index = lax.broadcasted_iota(jnp.int32, both.shape, 0) + start
            both = jnp.where(index < length, both, 0.0)
        out[z, here, :] = both.astype(out.dtype)

    return add


def first_kernel(prefix, lens, x, own, par, pos_k, pos_q, dq, part_own, part_par, queries, grads, lse_delta, dq_t):
    span = own.shape[0] - prefix
    load_rows(x, queries, grads, lse_delta)
    dq_t[...] = jnp.zeros_like(dq_t)
    rows = (queries, grads, lse_delta, dq_t)
    visit_shard(prefix, lens[1], par, pos_k[span:, :], pos_q, *rows, collect(prefix, lens[1], None, part_par))
    visit_shard(prefix, lens[0], own, pos_k[:span, :], pos_q, *rows, collect(prefix, lens[0], None, part_own))
    store_query_grad(dq_t, dq, x.shape[1] - AUX)


def second_kernel(prefix, lens, x, par, pos_k, pos_q, before, dq_t, part_par, queries, grads, lse_delta):
    span = par.shape[0] - prefix
    load_rows(x, queries, grads, lse_delta)
    dq_t[...] = jnp.zeros_like(dq_t)
    rows = (queries, grads, lse_delta, dq_t)
    visit_shard(prefix, lens[1], par, pos_k[span:, :], pos_q, *rows, collect(prefix, lens[1], before, part_par))


def third_kernel(
    prefix, lens, x, own, pos_k, pos_q, before, dq_in, arrived, dq, part_own, query_part, queries, grads, lse_delta, dq_t
):
    span = own.shape[0] - prefix
    load_rows(x, queries, grads, lse_delta)
    dq_t[...] = dq_in[...]
    rows = (queries, grads, lse_delta, dq_t)
    visit_shard(prefix, lens[0], own, pos_k[:span, :], pos_q, *rows, collect(prefix, lens[0], before, part_own))
    store_query_grad(dq_t, dq, x.shape[1] - AUX)
    query_part[...] = arrived[...].astype(F32).sum(0)


def call_kernel(kernel, flops, args, outs, scratch):
    vmem = pl.BlockSpec(memory_space=pltpu.VMEM)
    return pl.pallas_call(
        kernel,
        out_shape=outs,
        in_specs=[pl.BlockSpec(memory_space=pltpu.SMEM)] + [vmem] * (len(args) - 1),
        out_specs=(vmem,) * len(outs),
        scratch_shapes=[pltpu.VMEM(*s) for s in scratch],
        compiler_params=pltpu.CompilerParams(vmem_limit_bytes=VMEM_MIB * 2**20),
        cost_estimate=pl.CostEstimate(flops=flops, bytes_accessed=8 * 2**20, transcendentals=0),
    )(*args)


def split3(value):
    high = lax.reduce_precision(value, 8, 7)
    middle = lax.reduce_precision(value - high, 8, 7)
    low = value - high - middle
    return high.astype(BF16), middle.astype(BF16), low.astype(BF16)


def shards(
    n_ctx,
    n_head,
    queries,
    grad_out,
    saved_out,
    saved_lse,
    prefix_keys,
    prefix_values,
    span_keys,
    span_values,
    positions,
    prefix_len,
):
    heads_local = saved_lse.shape[0]
    rows_local = queries.shape[0]
    head_dim = queries.shape[1] // heads_local
    prefix = prefix_keys.shape[0]
    chips = n_ctx // 2
    rows = chips * rows_local
    me = lax.axis_index("ctx")
    core = lax.rem(me, 2)
    chip = me // 2
    same_core = [[2 * i + c for i in range(chips)] for c in range(2)]
    swap = [(i, i ^ 1) for i in range(n_ctx)]

    kv_own = jnp.concatenate(
        [jnp.concatenate([prefix_keys, span_keys], 0), jnp.concatenate([prefix_values, span_values], 0)], 1
    )
    kv_par = lax.ppermute(kv_own, "ctx", swap)
    lens = jnp.concatenate([prefix_len, lax.ppermute(prefix_len, "ctx", swap)])

    deltas = jnp.einsum(
        "ihd,ihd->hi",
        grad_out.reshape(rows_local, heads_local, head_dim),
        saved_out.reshape(rows_local, heads_local, head_dim),
        preferred_element_type=F32,
    )
    aux = jnp.stack(split3(jnp.concatenate([saved_lse * LOG2E, deltas], 1)))
    aux = jnp.pad(aux, ((0, AUX - 3), (0, 0), (0, 0)))

    by_core = positions.reshape(chips, 2, rows_local)
    pos_q = lax.dynamic_index_in_dim(by_core, core, 1, False).reshape(1, rows)
    pos_chip = lax.dynamic_index_in_dim(by_core, chip, 0, False)
    pos_k = jnp.where(core == 0, pos_chip, pos_chip[::-1]).reshape(2 * rows_local, 1)

    gathered = []
    for h in range(heads_local):
        columns = slice(h * head_dim, (h + 1) * head_dim)
        packed = jnp.concatenate(
            [aux[:, h], jnp.concatenate([queries[:, columns], grad_out[:, columns]], 1)], 0
        )
        sent = jnp.broadcast_to(packed[None], (chips,) + packed.shape)
        gathered.append(lax.all_to_all(sent, "ctx", 0, 0, axis_index_groups=same_core, tiled=True))

    dq_type = jax.ShapeDtypeStruct((rows, head_dim), BF16)
    part_type = jax.ShapeDtypeStruct((n_head, (prefix + rows_local) // n_head, 2 * head_dim), BF16)
    scratch = [((rows, head_dim), BF16)] * 2 + [((2, rows), F32), ((head_dim, rows), F32)]
    flops = 60 * rows * head_dim * (prefix + rows_local)
    def spread(dq):
        arrived = lax.all_to_all(dq, "ctx", 0, 0, axis_index_groups=same_core, tiled=True)
        return arrived.reshape(chips, rows_local, head_dim)

    dq, part_own, part_par = call_kernel(
        functools.partial(first_kernel, prefix),
        flops,
        (lens, gathered[0], kv_own, kv_par, pos_k, pos_q),
        (dq_type, part_type, part_type),
        scratch,
    )
    arrived = spread(dq)
    dq_t, part_par = call_kernel(
        functools.partial(second_kernel, prefix),
        flops // 2,
        (lens, gathered[1], kv_par, pos_k, pos_q, part_par),
        (jax.ShapeDtypeStruct((head_dim, rows), F32), part_type),
        scratch[:3],
    )
    returned = lax.ppermute(part_par, "ctx", swap)
    dq, part_own, query_part = call_kernel(
        functools.partial(third_kernel, prefix),
        flops // 2,
        (lens, gathered[1], kv_own, pos_k, pos_q, part_own, dq_t, arrived),
        (dq_type, part_type, jax.ShapeDtypeStruct((rows_local, head_dim), F32)),
        scratch,
    )
    both = (part_own.astype(F32) + returned.astype(F32)).astype(BF16)
    z = lax.axis_index("head")
    total = lax.dynamic_index_in_dim(both, z, 0, False).astype(F32)
    for hop in (1, n_head - 1, 2):
        sent = lax.dynamic_index_in_dim(both, lax.rem(z + hop, n_head), 0, False)
        total += lax.ppermute(sent, "head", [(i, (i + hop) % n_head) for i in range(n_head)]).astype(F32)
    query_grad = jnp.concatenate([query_part, spread(dq).astype(F32).sum(0)], 1)
    part = prefix // n_head
    return (
        query_grad,
        total[:part, :head_dim],
        total[:part, head_dim:],
        total[part:, :head_dim],
        total[part:, head_dim:],
    )


def solution(mesh):
    in_specs = (
        P("ctx", "head"),
        P("ctx", "head"),
        P("ctx", "head"),
        P("head", "ctx"),
        P("ctx", None),
        P("ctx", None),
        P("ctx", None),
        P("ctx", None),
        P(),
        P("ctx"),
    )
    out_specs = (
        P("ctx", "head"),
        P(("ctx", "head"), None),
        P(("ctx", "head"), None),
        P(("ctx", "head"), None),
        P(("ctx", "head"), None),
    )
    body = functools.partial(shards, mesh.shape["ctx"], mesh.shape["head"])
    return jax.shard_map(body, mesh=mesh, in_specs=in_specs, out_specs=out_specs, check_vma=False)
```

```python
import functools
import math

import jax
import jax.numpy as jnp
from jax import lax
from jax.experimental import pallas as pl
from jax.experimental.pallas import tpu as pltpu
from jax.sharding import PartitionSpec as P

BF16 = jnp.bfloat16
F32 = jnp.float32
AUX = 16
LOG2E = math.log2(math.e)
BLOCK = 512
ROW_BLOCK = 2048
VMEM_MIB = 40


def contract(a, b, dim_a, dim_b):
    return lax.dot_general(a, b, (((dim_a,), (dim_b,)), ((), ())), preferred_element_type=F32)


def load_rows(x, queries, grads, lse_delta):
    groups, rows_src, head_dim = x.shape[0], x.shape[1] - AUX, queries.shape[1]
    heads = x.shape[2] // (2 * head_dim)
    for s in range(groups):
        pieces = x[s, :AUX, :].astype(F32)
        total = pieces[0:1] + pieces[1:2] + pieces[2:3]
        for h in range(heads):
            here = pl.ds((h * groups + s) * rows_src, rows_src)
            at_query, at_grad = h * head_dim, (heads + h) * head_dim
            queries[here, :] = x[s, AUX:, at_query:at_query + head_dim]
            grads[here, :] = x[s, AUX:, at_grad:at_grad + head_dim]
            lse_delta[0:1, here] = total[:, at_query:at_query + rows_src]
            lse_delta[1:2, here] = total[:, at_grad:at_grad + rows_src]


def attention_kernel(
    prefix, lens, x, own, par, pos_k, pos_q, dq, part_own, part_par, queries, grads, lse_delta, dq_t, shards_kv, parts, sems
):
    rows, head_dim = queries.shape
    rows_chip, rows_src = pos_q.shape[1], x.shape[1] - AUX
    span = own.shape[0] - prefix
    heads_z = parts.shape[1]
    part, part_span = prefix // heads_z, span // heads_z
    scale = head_dim ** -0.5
    half = BLOCK // 2

    loads = [pltpu.make_async_copy(kv, shards_kv.at[i], sems.at[i]) for i, kv in enumerate((own, par))]
    stores = [pltpu.make_async_copy(parts.at[i], out, sems.at[2 + i]) for i, out in enumerate((part_own, part_par))]
    for copy in loads:
        copy.start()
    load_rows(x, queries, grads, lse_delta)
    loads[0].wait()
    dq_t[...] = jnp.zeros_like(dq_t)
    parts[...] = jnp.zeros_like(parts)

    def visit_shard(shard, carry):
        @pl.when(shard == 1)
        def _():
            loads[1].wait()
            stores[0].start()

        length = lens[shard]
        kv = shards_kv.at[shard]

        def gradients(start, width, causal, masked):
            here = pl.ds(start, width)
            keys, values = kv[here, :head_dim], kv[here, head_dim:]
            if masked:
                index = lax.broadcasted_iota(jnp.int32, (width, head_dim), 0) + start
                keys = jnp.where(index < length, keys, jnp.zeros((), BF16))
                values = jnp.where(index < length, values, jnp.zeros((), BF16))
            key_grad, value_grad = 0.0, 0.0
            for i in range(rows // ROW_BLOCK):
                some = pl.ds(i * ROW_BLOCK, ROW_BLOCK)
                query, grad = queries[some, :], grads[some, :]
                logits = contract(keys, query, 1, 1)
                probs = jnp.exp2(logits * (scale * LOG2E) - lse_delta[0:1, some])
                if causal:
                    begin = i * ROW_BLOCK % rows_chip
                    key_at = pos_k[pl.ds(pl.multiple_of(shard * span, span), span), :]
                    probs = jnp.where(key_at <= pos_q[0:1, begin:begin + ROW_BLOCK], probs, 0.0)
                dot_grad = contract(values, grad, 1, 1)
                score_low = (probs * (dot_grad - lse_delta[1:2, some])).astype(BF16)
                value_grad += contract(probs.astype(BF16), grad, 1, 0)
                key_grad += contract(score_low, query, 1, 0)
                dq_t[:, some] += contract(keys, score_low, 0, 0)
            return jnp.concatenate([key_grad * scale, value_grad], 1)

        def step(start, width, masked):
            both = gradients(start, width, False, masked)
            if masked:
                index = lax.broadcasted_iota(jnp.int32, both.shape, 0) + start
                both = jnp.where(index < length, both, 0.0)
            inside = pl.ds(pl.multiple_of(lax.rem(start, part), half), width)
            parts[shard, start // part, inside, :] = both.astype(BF16)

        both = gradients(prefix, span, True, False)
        for z in range(heads_z):
            parts[shard, z, part:, :] = both[z * part_span:(z + 1) * part_span].astype(BF16)

        wholes = length // BLOCK

        def whole(i, inner):
            step(pl.multiple_of(i * BLOCK, BLOCK), BLOCK, False)
            return inner

        lax.fori_loop(0, wholes, whole, 0)

        def remainder(i, inner):
            step(pl.multiple_of(i * half, half), half, True)
            return inner

        lax.fori_loop(2 * wholes, (length + half - 1) // half, remainder, 0)
        return carry

    lax.fori_loop(0, 2, visit_shard, 0)
    stores[1].start()
    for h in range(rows // rows_chip):
        for s in range(rows_chip // rows_src):
            here = pl.ds(h * rows_chip + s * rows_src, rows_src)
            dq[s, h * head_dim:(h + 1) * head_dim, :] = (dq_t[:, here] * scale).astype(BF16)
    for copy in stores:
        copy.wait()


def call_kernel(kernel, flops, args, outs, scratch):
    vmem, anywhere = pl.BlockSpec(memory_space=pltpu.VMEM), pl.BlockSpec(memory_space=pl.ANY)
    return pl.pallas_call(
        kernel,
        out_shape=outs,
        in_specs=[pl.BlockSpec(memory_space=pltpu.SMEM), vmem, anywhere, anywhere, vmem, vmem],
        out_specs=(vmem, anywhere, anywhere),
        scratch_shapes=[pltpu.VMEM(*s) for s in scratch] + [pltpu.SemaphoreType.DMA((4,))],
        compiler_params=pltpu.CompilerParams(vmem_limit_bytes=VMEM_MIB * 2**20),
        cost_estimate=pl.CostEstimate(flops=flops, bytes_accessed=8 * 2**20, transcendentals=0),
    )(*args)


def pack_kernel(queries, grad_out, saved_out, lse, sent):
    heads, rows = lse.shape
    head_dim = queries.shape[1] // heads
    deltas = []
    for h in range(heads):
        columns = slice(h * head_dim, (h + 1) * head_dim)
        product = grad_out[:, columns].astype(F32) * saved_out[:, columns].astype(F32)
        deltas.append(jnp.sum(product.T, 0, keepdims=True))
    values = jnp.concatenate([lse[h:h + 1, :] * LOG2E for h in range(heads)] + deltas, 1)
    pieces = []
    for _ in range(3):
        pieces.append(values.astype(BF16))
        values = values - pieces[-1].astype(F32)
    row = lax.broadcasted_iota(jnp.int32, (AUX, values.shape[1]), 0)
    aux = jnp.zeros(row.shape, F32)
    for i, piece in enumerate(pieces):
        aux = jnp.where(row == i, piece.astype(F32), aux)
    aux = aux.astype(BF16)
    for s in range(sent.shape[0]):
        sent[s, :AUX, :] = aux
        sent[s, AUX:, :heads * head_dim] = queries[...]
        sent[s, AUX:, heads * head_dim:] = grad_out[...]


def add_kernel(place, own, returned, *outs):
    for hop, out in zip(hops(own.shape[0]), outs):
        z = lax.rem(place[0] + hop, own.shape[0])
        out[...] = (own[z].astype(F32) + returned[z].astype(F32)).astype(BF16)


def sum_kernel(*refs):
    terms, outs = refs[:-4], refs[-4:]
    total = terms[0][...].astype(F32)
    for term in terms[1:]:
        total += term[...].astype(F32)
    part, head_dim = outs[0].shape
    outs[0][...] = total[:part, :head_dim]
    outs[1][...] = total[:part, head_dim:]
    outs[2][...] = total[part:, :head_dim]
    outs[3][...] = total[part:, head_dim:]


def hops(n_head):
    return [0, 1, n_head - 1] + list(range(2, n_head - 1))


def shards(
    n_ctx,
    n_head,
    queries,
    grad_out,
    saved_out,
    saved_lse,
    prefix_keys,
    prefix_values,
    span_keys,
    span_values,
    positions,
    prefix_len,
):
    heads_local = saved_lse.shape[0]
    rows_local = queries.shape[0]
    head_dim = queries.shape[1] // heads_local
    prefix = prefix_keys.shape[0]
    chips = n_ctx // 2
    rows = chips * rows_local
    me = lax.axis_index("ctx")
    core = lax.rem(me, 2)
    chip = me // 2
    same_core = [[2 * i + c for i in range(chips)] for c in range(2)]
    swap = [(i, i ^ 1) for i in range(n_ctx)]

    kv_own = jnp.concatenate(
        [jnp.concatenate([prefix_keys, span_keys], 0), jnp.concatenate([prefix_values, span_values], 0)], 1
    )
    kv_par = lax.ppermute(kv_own, "ctx", swap)
    lens = jnp.concatenate([prefix_len, lax.ppermute(prefix_len, "ctx", swap)])

    by_core = positions.reshape(chips, 2, rows_local)
    pos_q = lax.dynamic_index_in_dim(by_core, core, 1, False).reshape(1, rows)
    pos_chip = lax.dynamic_index_in_dim(by_core, chip, 0, False)
    pos_k = jnp.where(core == 0, pos_chip, pos_chip[::-1]).reshape(2 * rows_local, 1)

    vmem = pl.BlockSpec(memory_space=pltpu.VMEM)
    sent = pl.pallas_call(
        pack_kernel,
        out_shape=jax.ShapeDtypeStruct((chips, AUX + rows_local, 2 * queries.shape[1]), BF16),
        in_specs=[vmem] * 4,
        out_specs=vmem,
        compiler_params=pltpu.CompilerParams(vmem_limit_bytes=VMEM_MIB * 2**20),
    )(queries, grad_out, saved_out, saved_lse)
    gathered = lax.all_to_all(sent, "ctx", 0, 0, axis_index_groups=same_core, tiled=True)

    part_type = jax.ShapeDtypeStruct((n_head, (prefix + rows_local) // n_head, 2 * head_dim), BF16)
    dq, part_own, part_par = call_kernel(
        functools.partial(attention_kernel, prefix),
        60 * heads_local * rows * head_dim * (prefix + rows_local),
        (lens, gathered, kv_own, kv_par, pos_k, pos_q),
        (
            jax.ShapeDtypeStruct((chips, heads_local * head_dim, rows_local), BF16),
            part_type,
            part_type,
        ),
        [((heads_local * rows, head_dim), BF16)] * 2
        + [((2, heads_local * rows), F32), ((head_dim, heads_local * rows), F32)]
        + [((2,) + kv_own.shape, BF16), ((2,) + part_type.shape, BF16)],
    )
    arrived = lax.all_to_all(dq, "ctx", 0, 0, axis_index_groups=same_core, tiled=True)
    query_grad = arrived.astype(F32).sum(0).T
    returned = lax.ppermute(part_par, "ctx", swap)
    block = jax.ShapeDtypeStruct(part_type.shape[1:], BF16)
    params = pltpu.CompilerParams(vmem_limit_bytes=VMEM_MIB * 2**20)
    ready = pl.pallas_call(
        add_kernel,
        out_shape=(block,) * n_head,
        in_specs=[pl.BlockSpec(memory_space=pltpu.SMEM), vmem, vmem],
        out_specs=(vmem,) * n_head,
        compiler_params=params,
    )(lax.axis_index("head").astype(jnp.int32).reshape(1), part_own, returned)
    terms = [ready[0]]
    for hop, sent in zip(hops(n_head)[1:], ready[1:]):
        terms.append(lax.ppermute(sent, "head", [(i, (i + hop) % n_head) for i in range(n_head)]))
    prefix_type = jax.ShapeDtypeStruct((prefix // n_head, head_dim), F32)
    span_type = jax.ShapeDtypeStruct((rows_local // n_head, head_dim), F32)
    sums = pl.pallas_call(
        sum_kernel,
        out_shape=(prefix_type, prefix_type, span_type, span_type),
        in_specs=[vmem] * n_head,
        out_specs=(vmem,) * 4,
        compiler_params=params,
    )(*terms)
    return (query_grad, *sums)


def solution(mesh):
    in_specs = (
        P("ctx", "head"),
        P("ctx", "head"),
        P("ctx", "head"),
        P("head", "ctx"),
        P("ctx", None),
        P("ctx", None),
        P("ctx", None),
        P("ctx", None),
        P(),
        P("ctx"),
    )
    out_specs = (
        P("ctx", "head"),
        P(("ctx", "head"), None),
        P(("ctx", "head"), None),
        P(("ctx", "head"), None),
        P(("ctx", "head"), None),
    )
    body = functools.partial(shards, mesh.shape["ctx"], mesh.shape["head"])
    return jax.shard_map(body, mesh=mesh, in_specs=in_specs, out_specs=out_specs, check_vma=False)
```

```python
import functools
import math

import jax
import jax.numpy as jnp
from jax import lax
from jax.experimental import pallas as pl
from jax.experimental.pallas import tpu as pltpu
from jax.sharding import PartitionSpec as P

BF16 = jnp.bfloat16
F32 = jnp.float32
AUX = 16
LOG2E = math.log2(math.e)
BLOCK = 512
ROW_BLOCK = 1024
VMEM_MIB = 40
ALONE_MIB = 63


def contract(a, b, dim_a, dim_b):
    return lax.dot_general(a, b, (((dim_a,), (dim_b,)), ((), ())), preferred_element_type=F32)


def load_rows(x, queries, grads, lse_delta):
    groups, rows_src, head_dim = x.shape[0], x.shape[1] - AUX, queries.shape[1]
    heads = x.shape[2] // (2 * head_dim)
    for s in range(groups):
        pieces = x[s, :AUX, :].astype(F32)
        total = pieces[0:1] + pieces[1:2] + pieces[2:3]
        for h in range(heads):
            here = pl.ds((h * groups + s) * rows_src, rows_src)
            at_query, at_grad = h * head_dim, (heads + h) * head_dim
            queries[here, :] = x[s, AUX:, at_query:at_query + head_dim]
            grads[here, :] = x[s, AUX:, at_grad:at_grad + head_dim]
            lse_delta[0:1, here] = total[:, at_query:at_query + rows_src]
            lse_delta[1:2, here] = total[:, at_grad:at_grad + rows_src]


def attention_kernel(
    prefix, place, x, prefix_keys, prefix_values, span_keys, span_values, par, positions, dq, part_own, part_par,
    queries, grads, lse_delta, dq_t, shards_kv, parts, dq_block, pos_q, sems,
):
    rows, head_dim = queries.shape
    rows_chip, rows_src = pos_q.shape[1], x.shape[1] - AUX
    span = par.shape[0] - prefix
    heads_z = parts.shape[1]
    part, part_span = prefix // heads_z, span // heads_z
    scale = head_dim ** -0.5
    half, quarter = BLOCK // 2, BLOCK // 4

    loads = []
    for source, begin, column in (
        (prefix_keys, 0, 0), (prefix_values, 0, head_dim), (span_keys, prefix, 0), (span_values, prefix, head_dim)
    ):
        target = shards_kv.at[0, pl.ds(begin, source.shape[0]), pl.ds(column, head_dim)]
        loads.append(pltpu.make_async_copy(source, target, sems.at[len(loads)]))
    loads.append(pltpu.make_async_copy(par, shards_kv.at[1], sems.at[4]))
    stores = [pltpu.make_async_copy(parts.at[i], out, sems.at[5 + i]) for i, out in enumerate((part_own, part_par))]
    for copy in loads:
        copy.start()
    me, core = place[2], lax.rem(place[2], 2)
    for s in range(x.shape[0]):
        pos_q[0:1, s * rows_src:(s + 1) * rows_src] = positions[pl.ds(2 * s + core, 1), :].astype(F32)
    load_rows(x, queries, grads, lse_delta)
    for copy in loads[:4]:
        copy.wait()
    dq_t[...] = jnp.zeros_like(dq_t)
    parts[...] = jnp.zeros_like(parts)

    def visit_shard(shard, carry):
        @pl.when(shard == 1)
        def _():
            loads[4].wait()
            stores[0].start()

        length = place[shard]
        kv = shards_kv.at[shard]

        def gradients(start, width, causal, masked):
            here = pl.ds(start, width)
            keys, values = kv[here, :head_dim], kv[here, head_dim:]
            if masked:
                index = lax.broadcasted_iota(jnp.int32, (width, head_dim), 0) + start
                keys = jnp.where(index < length, keys, jnp.zeros((), BF16))
                values = jnp.where(index < length, values, jnp.zeros((), BF16))
            key_grad, value_grad = 0.0, 0.0
            for i in range(rows // ROW_BLOCK):
                some = pl.ds(i * ROW_BLOCK, ROW_BLOCK)
                query, grad = queries[some, :], grads[some, :]
                logits = contract(keys, query, 1, 1)
                probs = jnp.exp2(logits * (scale * LOG2E) - lse_delta[0:1, some])
                if causal:
                    begin = i * ROW_BLOCK % rows_chip
                    key_row = positions[pl.ds(me + shard * (1 - 2 * core), 1), :].astype(F32)
                    key_at = jnp.broadcast_to(key_row, (span, span)).T[:, 0:1]
                    probs = jnp.where(key_at <= pos_q[0:1, begin:begin + ROW_BLOCK], probs, 0.0)
                dot_grad = contract(values, grad, 1, 1)
                score_low = (probs * (dot_grad - lse_delta[1:2, some])).astype(BF16)
                value_grad += contract(probs.astype(BF16), grad, 1, 0)
                key_grad += contract(score_low, query, 1, 0)
                dq_t[:, some] += contract(keys, score_low, 0, 0)
            return jnp.concatenate([key_grad * scale, value_grad], 1)

        def step(start, width, masked):
            both = gradients(start, width, False, masked)
            if masked:
                index = lax.broadcasted_iota(jnp.int32, both.shape, 0) + start
                both = jnp.where(index < length, both, 0.0)
            inside = pl.ds(pl.multiple_of(lax.rem(start, part), quarter), width)
            parts[shard, start // part, inside, :] = both.astype(BF16)

        both = gradients(prefix, span, True, False)
        for z in range(heads_z):
            parts[shard, z, part:, :] = both[z * part_span:(z + 1) * part_span].astype(BF16)

        wholes = length // BLOCK

        def whole(i, inner):
            step(pl.multiple_of(i * BLOCK, BLOCK), BLOCK, False)
            return inner

        lax.fori_loop(0, wholes, whole, 0)

        pieces = (length + quarter - 1) // quarter

        def remainder(i, inner):
            step(pl.multiple_of(i * half, half), half, True)
            return inner

        lax.fori_loop(2 * wholes, pieces // 2, remainder, 0)

        @pl.when(lax.rem(pieces, 2) == 1)
        def _():
            step(pl.multiple_of((pieces - 1) * quarter, quarter), quarter, True)

        return carry

    lax.fori_loop(0, 2, visit_shard, 0)
    stores[1].start()
    for s in range(x.shape[0]):
        for h in range(rows // rows_chip):
            here = pl.ds(h * rows_chip + s * rows_src, rows_src)
            dq_block[s, h * head_dim:(h + 1) * head_dim, :] = (dq_t[:, here] * scale).astype(BF16)
        stores.append(pltpu.make_async_copy(dq_block.at[s], dq.at[s], sems.at[7 + s]))
        stores[-1].start()
    for copy in stores:
        copy.wait()


def pack_kernel(queries_in, grad_in, saved_in, lse_in, sent, queries, grad_out, saved_out, lse, block, sems):
    loads = []
    for source, target in ((queries_in, queries), (grad_in, grad_out), (saved_in, saved_out), (lse_in, lse)):
        loads.append(pltpu.make_async_copy(source, target, sems.at[len(loads)]))
        loads[-1].start()
    for copy in loads:
        copy.wait()
    heads, rows = lse.shape
    head_dim = queries.shape[1] // heads
    deltas = []
    for h in range(heads):
        columns = slice(h * head_dim, (h + 1) * head_dim)
        product = grad_out[:, columns].astype(F32) * saved_out[:, columns].astype(F32)
        deltas.append(jnp.sum(product.T, 0, keepdims=True))
    values = jnp.concatenate([lse[h:h + 1, :] * LOG2E for h in range(heads)] + deltas, 1)
    pieces = []
    for _ in range(3):
        pieces.append(values.astype(BF16))
        values = values - pieces[-1].astype(F32)
    row = lax.broadcasted_iota(jnp.int32, (AUX, values.shape[1]), 0)
    aux = jnp.zeros(row.shape, F32)
    for i, piece in enumerate(pieces):
        aux = jnp.where(row == i, piece.astype(F32), aux)
    aux = aux.astype(BF16)
    block[:AUX, :] = aux
    block[AUX:, :heads * head_dim] = queries[...]
    block[AUX:, heads * head_dim:] = grad_out[...]
    stores = [pltpu.make_async_copy(block, sent.at[s], sems.at[4 + s]) for s in range(sent.shape[0])]
    for copy in stores:
        copy.start()
    for copy in stores:
        copy.wait()


def reduce_kernel(arrived, out):
    out[...] = arrived[...].astype(F32).sum(0).T


def add_kernel(place, own, returned, *outs):
    for hop, out in zip(hops(own.shape[0]), outs):
        z = lax.rem(place[0] + hop, own.shape[0])
        out[...] = (own[z].astype(F32) + returned[z].astype(F32)).astype(BF16)


def sum_kernel(*refs):
    terms, outs = refs[:-4], refs[-4:]
    total = terms[0][...].astype(F32)
    for term in terms[1:]:
        total += term[...].astype(F32)
    part, head_dim = outs[0].shape
    outs[0][...] = total[:part, :head_dim]
    outs[1][...] = total[:part, head_dim:]
    outs[2][...] = total[part:, :head_dim]
    outs[3][...] = total[part:, head_dim:]


def hops(n_head):
    return [0, 1, n_head - 1] + list(range(2, n_head - 1))


def shards(
    n_ctx,
    n_head,
    queries,
    grad_out,
    saved_out,
    saved_lse,
    prefix_keys,
    prefix_values,
    span_keys,
    span_values,
    positions,
    prefix_len,
):
    heads_local = saved_lse.shape[0]
    rows_local = queries.shape[0]
    head_dim = queries.shape[1] // heads_local
    prefix = prefix_keys.shape[0]
    chips = n_ctx // 2
    rows = chips * rows_local
    me = lax.axis_index("ctx")
    same_core = [[2 * i + c for i in range(chips)] for c in range(2)]
    swap = [(i, i ^ 1) for i in range(n_ctx)]

    kv_own = jnp.concatenate(
        [jnp.concatenate([prefix_keys, span_keys], 0), jnp.concatenate([prefix_values, span_values], 0)], 1
    )
    kv_par = lax.ppermute(kv_own, "ctx", swap)
    place = jnp.concatenate([prefix_len, lax.ppermute(prefix_len, "ctx", swap), me.astype(jnp.int32).reshape(1)])

    smem, vmem, hbm = (pl.BlockSpec(memory_space=m) for m in (pltpu.SMEM, pltpu.VMEM, pltpu.HBM))
    params = pltpu.CompilerParams(vmem_limit_bytes=VMEM_MIB * 2**20)
    alone = pltpu.CompilerParams(vmem_limit_bytes=ALONE_MIB * 2**20)
    sent_type = jax.ShapeDtypeStruct((chips, AUX + rows_local, 2 * queries.shape[1]), BF16)
    sent = pl.pallas_call(
        pack_kernel,
        out_shape=sent_type,
        in_specs=[hbm] * 4,
        out_specs=hbm,
        scratch_shapes=[pltpu.VMEM(a.shape, a.dtype) for a in (queries, grad_out, saved_out, saved_lse)]
        + [pltpu.VMEM(sent_type.shape[1:], BF16), pltpu.SemaphoreType.DMA((4 + chips,))],
        compiler_params=alone,
    )(queries, grad_out, saved_out, saved_lse)
    gathered = lax.all_to_all(sent, "ctx", 0, 0, axis_index_groups=same_core, tiled=True)

    dq_type = jax.ShapeDtypeStruct((chips, heads_local * head_dim, rows_local), BF16)
    part_type = jax.ShapeDtypeStruct((n_head, (prefix + rows_local) // n_head, 2 * head_dim), BF16)
    all_rows = heads_local * rows
    dq, part_own, part_par = pl.pallas_call(
        functools.partial(attention_kernel, prefix),
        out_shape=(dq_type, part_type, part_type),
        in_specs=[smem, vmem] + [hbm] * 5 + [vmem],
        out_specs=(hbm, pl.BlockSpec(memory_space=pl.ANY), hbm),
        scratch_shapes=[
            pltpu.VMEM((all_rows, head_dim), BF16),
            pltpu.VMEM((all_rows, head_dim), BF16),
            pltpu.VMEM((2, all_rows), F32),
            pltpu.VMEM((head_dim, all_rows), F32),
            pltpu.VMEM((2,) + kv_own.shape, BF16),
            pltpu.VMEM((2,) + part_type.shape, BF16),
            pltpu.VMEM(dq_type.shape, BF16),
            pltpu.VMEM((1, rows), F32),
            pltpu.SemaphoreType.DMA((7 + chips,)),
        ],
        compiler_params=alone,
        cost_estimate=pl.CostEstimate(
            flops=60 * all_rows * head_dim * (prefix + rows_local), bytes_accessed=8 * 2**20, transcendentals=0
        ),
    )(
        place, gathered, prefix_keys, prefix_values, span_keys, span_values, kv_par,
        positions.reshape(n_ctx, rows_local),
    )
    arrived = lax.all_to_all(dq, "ctx", 0, 0, axis_index_groups=same_core, tiled=True)
    query_grad = pl.pallas_call(
        reduce_kernel,
        out_shape=jax.ShapeDtypeStruct(queries.shape, F32),
        in_specs=[vmem],
        out_specs=vmem,
        compiler_params=params,
    )(arrived)
    returned = lax.ppermute(part_par, "ctx", swap)
    block = jax.ShapeDtypeStruct(part_type.shape[1:], BF16)
    ready = pl.pallas_call(
        add_kernel,
        out_shape=(block,) * n_head,
        in_specs=[smem, vmem, vmem],
        out_specs=(vmem,) * n_head,
        compiler_params=params,
    )(lax.axis_index("head").astype(jnp.int32).reshape(1), part_own, returned)
    terms = [ready[0]]
    for hop, sent in zip(hops(n_head)[1:], ready[1:]):
        terms.append(lax.ppermute(sent, "head", [(i, (i + hop) % n_head) for i in range(n_head)]))
    prefix_type = jax.ShapeDtypeStruct((prefix // n_head, head_dim), F32)
    span_type = jax.ShapeDtypeStruct((rows_local // n_head, head_dim), F32)
    sums = pl.pallas_call(
        sum_kernel,
        out_shape=(prefix_type, prefix_type, span_type, span_type),
        in_specs=[vmem] * n_head,
        out_specs=(vmem,) * 4,
        compiler_params=params,
    )(*terms)
    return (query_grad, *sums)


def solution(mesh):
    in_specs = (
        P("ctx", "head"),
        P("ctx", "head"),
        P("ctx", "head"),
        P("head", "ctx"),
        P("ctx", None),
        P("ctx", None),
        P("ctx", None),
        P("ctx", None),
        P(),
        P("ctx"),
    )
    out_specs = (
        P("ctx", "head"),
        P(("ctx", "head"), None),
        P(("ctx", "head"), None),
        P(("ctx", "head"), None),
        P(("ctx", "head"), None),
    )
    body = functools.partial(shards, mesh.shape["ctx"], mesh.shape["head"])
    return jax.shard_map(body, mesh=mesh, in_specs=in_specs, out_specs=out_specs, check_vma=False)
```

```python
import functools
import math

import jax
import jax.numpy as jnp
from jax import lax
from jax.experimental import pallas as pl
from jax.experimental.pallas import tpu as pltpu
from jax.sharding import PartitionSpec as P

BF16 = jnp.bfloat16
F32 = jnp.float32
AUX = 16
LOG2E = math.log2(math.e)
BLOCK = 512
ROW_BLOCK = 1024
VMEM_MIB = 40
ALONE_MIB = 63


def contract(a, b, dim_a, dim_b):
    return lax.dot_general(a, b, (((dim_a,), (dim_b,)), ((), ())), preferred_element_type=F32)


def load_scalars(x_aux, lse_delta, rows_src):
    groups, heads = x_aux.shape[0], lse_delta.shape[1] // (x_aux.shape[0] * rows_src)
    for s in range(groups):
        pieces = x_aux[s].astype(F32)
        count = 2 * heads
        total = pieces[:count] + pieces[count:2 * count] + pieces[2 * count:3 * count]
        for h in range(heads):
            here = pl.ds((h * groups + s) * rows_src, rows_src)
            lse_delta[0:1, here] = total[h:h + 1]
            lse_delta[1:2, here] = total[heads + h:heads + h + 1]


def attention_kernel(
    prefix, place, x_in, prefix_keys, prefix_values, span_keys, span_values, par, positions_in, dq, part_own, part_par,
    x_aux, positions, queries, grads, lse_delta, dq_t, shards_kv, parts, dq_block, pos_q, sems,
):
    heads, groups, rows_src, head_dim = queries.shape
    rows_chip = groups * rows_src
    rows = heads * rows_chip
    span = par.shape[0] - prefix
    heads_z = parts.shape[1]
    part, part_span = prefix // heads_z, span // heads_z
    scale = head_dim ** -0.5
    half, quarter = BLOCK // 2, BLOCK // 4

    pairs = [(positions_in, positions), (x_in.at[:, pl.ds(2 * heads * rows_src, AUX), :], x_aux)]
    for h in range(heads):
        pairs.append((x_in.at[:, pl.ds(h * rows_src, rows_src), :], queries.at[h]))
        pairs.append((x_in.at[:, pl.ds((heads + h) * rows_src, rows_src), :], grads.at[h]))
    for source, begin, column in (
        (prefix_keys, 0, 0), (prefix_values, 0, head_dim), (span_keys, prefix, 0), (span_values, prefix, head_dim)
    ):
        pairs.append((source, shards_kv.at[0, pl.ds(begin, source.shape[0]), pl.ds(column, head_dim)]))
    pairs.append((par, shards_kv.at[1]))
    loads = [pltpu.make_async_copy(*pair, sems.at[i]) for i, pair in enumerate(pairs)]
    stores = [pltpu.make_async_copy(parts.at[i], out, sems.at[len(loads) + i]) for i, out in enumerate((part_own, part_par))]
    for copy in loads:
        copy.start()
    dq_t[...] = jnp.zeros_like(dq_t)
    parts[...] = jnp.zeros_like(parts)
    for copy in loads[:2]:
        copy.wait()
    me, core = place[2], lax.rem(place[2], 2)
    for s in range(groups):
        pos_q[0:1, s * rows_src:(s + 1) * rows_src] = positions[pl.ds(2 * s + core, 1), :].astype(F32)
    load_scalars(x_aux, lse_delta, rows_src)
    for copy in loads[2:]:
        copy.wait()

    def gradients(keys, values, key_at):
        key_grad, value_grad = 0.0, 0.0
        for i in range(rows // ROW_BLOCK):
            some = pl.ds(i * ROW_BLOCK, ROW_BLOCK)
            head, begin = i * ROW_BLOCK // rows_chip, i * ROW_BLOCK % rows_chip
            sources = pl.ds(begin // rows_src, ROW_BLOCK // rows_src)
            query = queries[head, sources].reshape(ROW_BLOCK, head_dim)
            grad = grads[head, sources].reshape(ROW_BLOCK, head_dim)
            logits = contract(keys, query, 1, 1)
            probs = jnp.exp2(logits * (scale * LOG2E) - lse_delta[0:1, some])
            if key_at is not None:
                probs = jnp.where(key_at <= pos_q[0:1, begin:begin + ROW_BLOCK], probs, 0.0)
            dot_grad = contract(values, grad, 1, 1)
            score_low = (probs * (dot_grad - lse_delta[1:2, some])).astype(BF16)
            value_grad += contract(probs.astype(BF16), grad, 1, 0)
            key_grad += contract(score_low, query, 1, 0)
            dq_t[:, some] += contract(keys, score_low, 0, 0)
        return jnp.concatenate([key_grad * scale, value_grad], 1)

    key_at = []
    for shard, ctx in ((0, me), (1, me + 1 - 2 * core)):
        key_row = positions[pl.ds(ctx, 1), :].astype(F32)
        key_at.append(jnp.broadcast_to(key_row, (span, span)).T[:, 0:1])
    span_kv = jnp.concatenate([shards_kv[0, prefix:, :], shards_kv[1, prefix:, :]], 0)
    both = gradients(span_kv[:, :head_dim], span_kv[:, head_dim:], jnp.concatenate(key_at, 0))
    for shard in range(2):
        for z in range(heads_z):
            begin = shard * span + z * part_span
            parts[shard, z, part:, :] = both[begin:begin + part_span].astype(BF16)

    def visit_shard(shard, carry):
        @pl.when(shard == 1)
        def _():
            stores[0].start()

        length = place[shard]
        kv = shards_kv.at[shard]

        def step(start, width, masked):
            here = pl.ds(start, width)
            keys, values = kv[here, :head_dim], kv[here, head_dim:]
            if masked:
                index = lax.broadcasted_iota(jnp.int32, (width, head_dim), 0) + start
                keys = jnp.where(index < length, keys, jnp.zeros((), BF16))
                values = jnp.where(index < length, values, jnp.zeros((), BF16))
            both = gradients(keys, values, None)
            if masked:
                index = lax.broadcasted_iota(jnp.int32, both.shape, 0) + start
                both = jnp.where(index < length, both, 0.0)
            inside = pl.ds(pl.multiple_of(lax.rem(start, part), quarter), width)
            parts[shard, start // part, inside, :] = both.astype(BF16)

        wholes = length // BLOCK

        def whole(i, inner):
            step(pl.multiple_of(i * BLOCK, BLOCK), BLOCK, False)
            return inner

        lax.fori_loop(0, wholes, whole, 0)
        pieces = (length + quarter - 1) // quarter

        def remainder(i, inner):
            step(pl.multiple_of(i * half, half), half, True)
            return inner

        lax.fori_loop(2 * wholes, pieces // 2, remainder, 0)

        @pl.when(lax.rem(pieces, 2) == 1)
        def _():
            step(pl.multiple_of((pieces - 1) * quarter, quarter), quarter, True)

        return carry

    lax.fori_loop(0, 2, visit_shard, 0)
    stores[1].start()
    for s in range(groups):
        for h in range(heads):
            here = pl.ds(h * rows_chip + s * rows_src, rows_src)
            dq_block[s, h * head_dim:(h + 1) * head_dim, :] = (dq_t[:, here] * scale).astype(BF16)
        stores.append(pltpu.make_async_copy(dq_block.at[s], dq.at[s], sems.at[len(loads) + len(stores)]))
        stores[-1].start()
    for copy in stores:
        copy.wait()


def pack_kernel(queries_in, grad_in, saved_in, lse_in, sent, queries, grad_out, saved_out, lse, block, sems):
    loads = []
    for source, target in ((queries_in, queries), (grad_in, grad_out), (saved_in, saved_out), (lse_in, lse)):
        loads.append(pltpu.make_async_copy(source, target, sems.at[len(loads)]))
        loads[-1].start()
    for copy in loads:
        copy.wait()
    heads, rows = lse.shape
    head_dim = queries.shape[1] // heads
    values = [lse[h:h + 1, :] * LOG2E for h in range(heads)]
    for h in range(heads):
        columns = slice(h * head_dim, (h + 1) * head_dim)
        product = grad_out[:, columns].astype(F32) * saved_out[:, columns].astype(F32)
        values.append(jnp.sum(product.T, 0, keepdims=True))
        block[h * rows:(h + 1) * rows, :] = queries[:, columns]
        block[(heads + h) * rows:(heads + h + 1) * rows, :] = grad_out[:, columns]
    row = lax.broadcasted_iota(jnp.int32, (AUX, rows), 0)
    aux = jnp.zeros(row.shape, F32)
    for j, value in enumerate(values):
        for i in range(3):
            piece = value.astype(BF16).astype(F32)
            value = value - piece
            aux = jnp.where(row == i * len(values) + j, piece, aux)
    block[2 * heads * rows:, :] = aux.astype(BF16)
    stores = [pltpu.make_async_copy(block, sent.at[s], sems.at[4 + s]) for s in range(sent.shape[0])]
    for copy in stores:
        copy.start()
    for copy in stores:
        copy.wait()


def add_kernel(place, own, returned, *outs):
    for hop, out in zip(hops(own.shape[0]), outs):
        z = lax.rem(place[0] + hop, own.shape[0])
        out[...] = (own[z].astype(F32) + returned[z].astype(F32)).astype(BF16)


def sum_kernel(arrived, *refs):
    terms, query_grad, outs = refs[:-5], refs[-5], refs[-4:]
    query_grad[...] = arrived[...].astype(F32).sum(0).T
    total = terms[0][...].astype(F32)
    for term in terms[1:]:
        total += term[...].astype(F32)
    part, head_dim = outs[0].shape
    outs[0][...] = total[:part, :head_dim]
    outs[1][...] = total[:part, head_dim:]
    outs[2][...] = total[part:, :head_dim]
    outs[3][...] = total[part:, head_dim:]


def hops(n_head):
    return [0, 1, n_head - 1] + list(range(2, n_head - 1))


def shards(
    n_ctx,
    n_head,
    queries,
    grad_out,
    saved_out,
    saved_lse,
    prefix_keys,
    prefix_values,
    span_keys,
    span_values,
    positions,
    prefix_len,
):
    heads_local = saved_lse.shape[0]
    rows_local = queries.shape[0]
    head_dim = queries.shape[1] // heads_local
    prefix = prefix_keys.shape[0]
    chips = n_ctx // 2
    rows = chips * rows_local
    me = lax.axis_index("ctx")
    same_core = [[2 * i + c for i in range(chips)] for c in range(2)]
    swap = [(i, i ^ 1) for i in range(n_ctx)]

    kv_own = jnp.concatenate(
        [jnp.concatenate([prefix_keys, span_keys], 0), jnp.concatenate([prefix_values, span_values], 0)], 1
    )
    kv_par = lax.ppermute(kv_own, "ctx", swap)
    place = jnp.concatenate([prefix_len, lax.ppermute(prefix_len, "ctx", swap), me.astype(jnp.int32).reshape(1)])

    smem, vmem, hbm = (pl.BlockSpec(memory_space=m) for m in (pltpu.SMEM, pltpu.VMEM, pltpu.HBM))
    params = pltpu.CompilerParams(vmem_limit_bytes=VMEM_MIB * 2**20)
    alone = pltpu.CompilerParams(vmem_limit_bytes=ALONE_MIB * 2**20)
    sent_type = jax.ShapeDtypeStruct((chips, 2 * heads_local * rows_local + AUX, head_dim), BF16)
    sent = pl.pallas_call(
        pack_kernel,
        out_shape=sent_type,
        in_specs=[hbm] * 4,
        out_specs=hbm,
        scratch_shapes=[pltpu.VMEM(a.shape, a.dtype) for a in (queries, grad_out, saved_out, saved_lse)]
        + [pltpu.VMEM(sent_type.shape[1:], BF16), pltpu.SemaphoreType.DMA((4 + chips,))],
        compiler_params=alone,
    )(queries, grad_out, saved_out, saved_lse)
    gathered = lax.all_to_all(sent, "ctx", 0, 0, axis_index_groups=same_core, tiled=True)

    dq_type = jax.ShapeDtypeStruct((chips, heads_local * head_dim, rows_local), BF16)
    part_type = jax.ShapeDtypeStruct((n_head, (prefix + rows_local) // n_head, 2 * head_dim), BF16)
    all_rows = heads_local * rows
    dq, part_own, part_par = pl.pallas_call(
        functools.partial(attention_kernel, prefix),
        out_shape=(dq_type, part_type, part_type),
        in_specs=[smem] + [hbm] * 7,
        out_specs=(hbm, pl.BlockSpec(memory_space=pl.ANY), hbm),
        scratch_shapes=[
            pltpu.VMEM((chips, AUX, head_dim), BF16),
            pltpu.VMEM((n_ctx, rows_local), jnp.int32),
            pltpu.VMEM((heads_local, chips, rows_local, head_dim), BF16),
            pltpu.VMEM((heads_local, chips, rows_local, head_dim), BF16),
            pltpu.VMEM((2, all_rows), F32),
            pltpu.VMEM((head_dim, all_rows), F32),
            pltpu.VMEM((2,) + kv_own.shape, BF16),
            pltpu.VMEM((2,) + part_type.shape, BF16),
            pltpu.VMEM(dq_type.shape, BF16),
            pltpu.VMEM((1, rows), F32),
            pltpu.SemaphoreType.DMA((9 + 2 * heads_local + chips,)),
        ],
        compiler_params=alone,
        cost_estimate=pl.CostEstimate(
            flops=60 * all_rows * head_dim * (prefix + rows_local), bytes_accessed=8 * 2**20, transcendentals=0
        ),
    )(
        place, gathered, prefix_keys, prefix_values, span_keys, span_values, kv_par,
        positions.reshape(n_ctx, rows_local),
    )
    arrived = lax.all_to_all(dq, "ctx", 0, 0, axis_index_groups=same_core, tiled=True)
    returned = lax.ppermute(part_par, "ctx", swap)
    block = jax.ShapeDtypeStruct(part_type.shape[1:], BF16)
    ready = pl.pallas_call(
        add_kernel,
        out_shape=(block,) * n_head,
        in_specs=[smem, vmem, vmem],
        out_specs=(vmem,) * n_head,
        compiler_params=params,
    )(lax.axis_index("head").astype(jnp.int32).reshape(1), part_own, returned)
    terms = [ready[0]]
    for hop, sent in zip(hops(n_head)[1:], ready[1:]):
        terms.append(lax.ppermute(sent, "head", [(i, (i + hop) % n_head) for i in range(n_head)]))
    prefix_type = jax.ShapeDtypeStruct((prefix // n_head, head_dim), F32)
    span_type = jax.ShapeDtypeStruct((rows_local // n_head, head_dim), F32)
    return pl.pallas_call(
        sum_kernel,
        out_shape=(jax.ShapeDtypeStruct(queries.shape, F32), prefix_type, prefix_type, span_type, span_type),
        in_specs=[vmem] * (1 + n_head),
        out_specs=(vmem,) * 5,
        compiler_params=params,
    )(arrived, *terms)


def solution(mesh):
    in_specs = (
        P("ctx", "head"),
        P("ctx", "head"),
        P("ctx", "head"),
        P("head", "ctx"),
        P("ctx", None),
        P("ctx", None),
        P("ctx", None),
        P("ctx", None),
        P(),
        P("ctx"),
    )
    out_specs = (
        P("ctx", "head"),
        P(("ctx", "head"), None),
        P(("ctx", "head"), None),
        P(("ctx", "head"), None),
        P(("ctx", "head"), None),
    )
    body = functools.partial(shards, mesh.shape["ctx"], mesh.shape["head"])
    return jax.shard_map(body, mesh=mesh, in_specs=in_specs, out_specs=out_specs, check_vma=False)
```

```python
import functools
import math

import jax
import jax.numpy as jnp
from jax import lax
from jax.experimental import pallas as pl
from jax.experimental.pallas import tpu as pltpu
from jax.sharding import PartitionSpec as P

BF16 = jnp.bfloat16
F32 = jnp.float32
AUX = 16
LOG2E = math.log2(math.e)
BLOCK = 512
ROW_BLOCK = 2048
VMEM_MIB = 40
ALONE_MIB = 63


def contract(a, b, dim_a, dim_b):
    return lax.dot_general(a, b, (((dim_a,), (dim_b,)), ((), ())), preferred_element_type=F32)


def load_scalars(x_aux, lse_delta, rows_src):
    groups, heads = x_aux.shape[0], lse_delta.shape[1] // (x_aux.shape[0] * rows_src)
    for s in range(groups):
        pieces = x_aux[s].astype(F32)
        count = 2 * heads
        total = pieces[:count] + pieces[count:2 * count] + pieces[2 * count:3 * count]
        for h in range(heads):
            here = pl.ds((h * groups + s) * rows_src, rows_src)
            lse_delta[0:1, here] = total[h:h + 1]
            lse_delta[1:2, here] = total[heads + h:heads + h + 1]


def attention_kernel(
    prefix, place, x_in, prefix_keys, prefix_values, span_keys, span_values, par, positions_in, dq, part_own, part_par,
    x_aux, positions, queries, grads, lse_delta, dq_t, shards_kv, parts, dq_block, pos_q, sems,
):
    heads, groups, rows_src, head_dim = queries.shape
    rows_chip = groups * rows_src
    rows = heads * rows_chip
    span = par.shape[0] - prefix
    heads_z = parts.shape[1]
    part, part_span = prefix // heads_z, span // heads_z
    scale = head_dim ** -0.5
    half, quarter = BLOCK // 2, BLOCK // 4

    pairs = [(positions_in, positions), (x_in.at[:, pl.ds(2 * heads * rows_src, AUX), :], x_aux)]
    for h in range(heads):
        pairs.append((x_in.at[:, pl.ds(h * rows_src, rows_src), :], queries.at[h]))
        pairs.append((x_in.at[:, pl.ds((heads + h) * rows_src, rows_src), :], grads.at[h]))
    for source, begin, column in (
        (prefix_keys, 0, 0), (prefix_values, 0, head_dim), (span_keys, prefix, 0), (span_values, prefix, head_dim)
    ):
        pairs.append((source, shards_kv.at[0, pl.ds(begin, source.shape[0]), pl.ds(column, head_dim)]))
    pairs.append((par, shards_kv.at[1]))
    loads = [pltpu.make_async_copy(*pair, sems.at[i]) for i, pair in enumerate(pairs)]
    stores = [pltpu.make_async_copy(parts.at[i], out, sems.at[len(loads) + i]) for i, out in enumerate((part_own, part_par))]
    for copy in loads:
        copy.start()
    dq_t[...] = jnp.zeros_like(dq_t)
    parts[...] = jnp.zeros_like(parts)
    for copy in loads[:2]:
        copy.wait()
    me, core = place[2], lax.rem(place[2], 2)
    for s in range(groups):
        pos_q[0:1, s * rows_src:(s + 1) * rows_src] = positions[pl.ds(2 * s + core, 1), :].astype(F32)
    load_scalars(x_aux, lse_delta, rows_src)
    for copy in loads[2:]:
        copy.wait()

    def gradients(keys, values, key_at):
        key_grad, value_grad = 0.0, 0.0
        held = []
        for i in range(rows // ROW_BLOCK):
            some = pl.ds(i * ROW_BLOCK, ROW_BLOCK)
            head, begin = i * ROW_BLOCK // rows_chip, i * ROW_BLOCK % rows_chip
            sources = pl.ds(begin // rows_src, ROW_BLOCK // rows_src)
            query = queries[head, sources].reshape(ROW_BLOCK, head_dim)
            grad = grads[head, sources].reshape(ROW_BLOCK, head_dim)
            logits = contract(keys, query, 1, 1)
            probs = jnp.exp2(logits * (scale * LOG2E) - lse_delta[0:1, some])
            if key_at is not None:
                probs = jnp.where(key_at <= pos_q[0:1, begin:begin + ROW_BLOCK], probs, 0.0)
            dot_grad = contract(values, grad, 1, 1)
            score_low = (probs * (dot_grad - lse_delta[1:2, some])).astype(BF16)
            value_grad += contract(probs.astype(BF16), grad, 1, 0)
            key_grad += contract(score_low, query, 1, 0)
            held.append((some, score_low))
        for some, score_low in held:
            dq_t[:, some] += contract(keys, score_low, 0, 0)
        return jnp.concatenate([key_grad * scale, value_grad], 1)

    key_at = []
    for shard, ctx in ((0, me), (1, me + 1 - 2 * core)):
        key_row = positions[pl.ds(ctx, 1), :].astype(F32)
        key_at.append(jnp.broadcast_to(key_row, (span, span)).T[:, 0:1])
    span_kv = jnp.concatenate([shards_kv[0, prefix:, :], shards_kv[1, prefix:, :]], 0)
    both = gradients(span_kv[:, :head_dim], span_kv[:, head_dim:], jnp.concatenate(key_at, 0))
    for shard in range(2):
        for z in range(heads_z):
            begin = shard * span + z * part_span
            parts[shard, z, part:, :] = both[begin:begin + part_span].astype(BF16)

    def visit_shard(shard, carry):
        @pl.when(shard == 1)
        def _():
            stores[0].start()

        length = place[shard]
        kv = shards_kv.at[shard]

        def step(start, width, masked):
            here = pl.ds(start, width)
            keys, values = kv[here, :head_dim], kv[here, head_dim:]
            if masked:
                index = lax.broadcasted_iota(jnp.int32, (width, head_dim), 0) + start
                keys = jnp.where(index < length, keys, jnp.zeros((), BF16))
                values = jnp.where(index < length, values, jnp.zeros((), BF16))
            both = gradients(keys, values, None)
            if masked:
                index = lax.broadcasted_iota(jnp.int32, both.shape, 0) + start
                both = jnp.where(index < length, both, 0.0)
            inside = pl.ds(pl.multiple_of(lax.rem(start, part), quarter), width)
            parts[shard, start // part, inside, :] = both.astype(BF16)

        wholes = length // BLOCK

        def whole(i, inner):
            step(pl.multiple_of(i * BLOCK, BLOCK), BLOCK, False)
            return inner

        lax.fori_loop(0, wholes, whole, 0)
        pieces = (length + quarter - 1) // quarter

        def remainder(i, inner):
            step(pl.multiple_of(i * half, half), half, True)
            return inner

        lax.fori_loop(2 * wholes, pieces // 2, remainder, 0)

        @pl.when(lax.rem(pieces, 2) == 1)
        def _():
            step(pl.multiple_of((pieces - 1) * quarter, quarter), quarter, True)

        return carry

    lax.fori_loop(0, 2, visit_shard, 0)
    stores[1].start()
    for s in range(groups):
        for h in range(heads):
            here = pl.ds(h * rows_chip + s * rows_src, rows_src)
            dq_block[s, h * head_dim:(h + 1) * head_dim, :] = (dq_t[:, here] * scale).astype(BF16)
        stores.append(pltpu.make_async_copy(dq_block.at[s], dq.at[s], sems.at[len(loads) + len(stores)]))
        stores[-1].start()
    for copy in stores:
        copy.wait()


def pack_kernel(queries_in, grad_in, saved_in, lse_in, sent, queries, grad_out, saved_out, lse, block, sems):
    loads = []
    for source, target in ((queries_in, queries), (grad_in, grad_out), (saved_in, saved_out), (lse_in, lse)):
        loads.append(pltpu.make_async_copy(source, target, sems.at[len(loads)]))
        loads[-1].start()
    for copy in loads:
        copy.wait()
    heads, rows = lse.shape
    head_dim = queries.shape[1] // heads
    values = [lse[h:h + 1, :] * LOG2E for h in range(heads)]
    for h in range(heads):
        columns = slice(h * head_dim, (h + 1) * head_dim)
        product = grad_out[:, columns].astype(F32) * saved_out[:, columns].astype(F32)
        values.append(jnp.sum(product.T, 0, keepdims=True))
        block[h * rows:(h + 1) * rows, :] = queries[:, columns]
        block[(heads + h) * rows:(heads + h + 1) * rows, :] = grad_out[:, columns]
    row = lax.broadcasted_iota(jnp.int32, (AUX, rows), 0)
    aux = jnp.zeros(row.shape, F32)
    for j, value in enumerate(values):
        for i in range(3):
            piece = value.astype(BF16).astype(F32)
            value = value - piece
            aux = jnp.where(row == i * len(values) + j, piece, aux)
    block[2 * heads * rows:, :] = aux.astype(BF16)
    stores = [pltpu.make_async_copy(block, sent.at[s], sems.at[4 + s]) for s in range(sent.shape[0])]
    for copy in stores:
        copy.start()
    for copy in stores:
        copy.wait()


def add_kernel(place, own, returned, *outs):
    for hop, out in zip(hops(own.shape[0]), outs):
        z = lax.rem(place[0] + hop, own.shape[0])
        out[...] = (own[z].astype(F32) + returned[z].astype(F32)).astype(BF16)


def sum_kernel(arrived, *refs):
    terms, query_grad, outs = refs[:-5], refs[-5], refs[-4:]
    query_grad[...] = arrived[...].astype(F32).sum(0).T
    total = terms[0][...].astype(F32)
    for term in terms[1:]:
        total += term[...].astype(F32)
    part, head_dim = outs[0].shape
    outs[0][...] = total[:part, :head_dim]
    outs[1][...] = total[:part, head_dim:]
    outs[2][...] = total[part:, :head_dim]
    outs[3][...] = total[part:, head_dim:]


def hops(n_head):
    return [0, 1, n_head - 1] + list(range(2, n_head - 1))


def shards(
    n_ctx,
    n_head,
    queries,
    grad_out,
    saved_out,
    saved_lse,
    prefix_keys,
    prefix_values,
    span_keys,
    span_values,
    positions,
    prefix_len,
):
    heads_local = saved_lse.shape[0]
    rows_local = queries.shape[0]
    head_dim = queries.shape[1] // heads_local
    prefix = prefix_keys.shape[0]
    chips = n_ctx // 2
    rows = chips * rows_local
    me = lax.axis_index("ctx")
    same_core = [[2 * i + c for i in range(chips)] for c in range(2)]
    swap = [(i, i ^ 1) for i in range(n_ctx)]

    kv_own = jnp.concatenate(
        [jnp.concatenate([prefix_keys, span_keys], 0), jnp.concatenate([prefix_values, span_values], 0)], 1
    )
    kv_par = lax.ppermute(kv_own, "ctx", swap)
    place = jnp.concatenate([prefix_len, lax.ppermute(prefix_len, "ctx", swap), me.astype(jnp.int32).reshape(1)])

    smem, vmem, hbm = (pl.BlockSpec(memory_space=m) for m in (pltpu.SMEM, pltpu.VMEM, pltpu.HBM))
    params = pltpu.CompilerParams(vmem_limit_bytes=VMEM_MIB * 2**20)
    alone = pltpu.CompilerParams(vmem_limit_bytes=ALONE_MIB * 2**20)
    sent_type = jax.ShapeDtypeStruct((chips, 2 * heads_local * rows_local + AUX, head_dim), BF16)
    sent = pl.pallas_call(
        pack_kernel,
        out_shape=sent_type,
        in_specs=[hbm] * 4,
        out_specs=hbm,
        scratch_shapes=[pltpu.VMEM(a.shape, a.dtype) for a in (queries, grad_out, saved_out, saved_lse)]
        + [pltpu.VMEM(sent_type.shape[1:], BF16), pltpu.SemaphoreType.DMA((4 + chips,))],
        compiler_params=alone,
    )(queries, grad_out, saved_out, saved_lse)
    gathered = lax.all_to_all(sent, "ctx", 0, 0, axis_index_groups=same_core, tiled=True)

    dq_type = jax.ShapeDtypeStruct((chips, heads_local * head_dim, rows_local), BF16)
    part_type = jax.ShapeDtypeStruct((n_head, (prefix + rows_local) // n_head, 2 * head_dim), BF16)
    all_rows = heads_local * rows
    dq, part_own, part_par = pl.pallas_call(
        functools.partial(attention_kernel, prefix),
        out_shape=(dq_type, part_type, part_type),
        in_specs=[smem] + [hbm] * 7,
        out_specs=(hbm, pl.BlockSpec(memory_space=pl.ANY), hbm),
        scratch_shapes=[
            pltpu.VMEM((chips, AUX, head_dim), BF16),
            pltpu.VMEM((n_ctx, rows_local), jnp.int32),
            pltpu.VMEM((heads_local, chips, rows_local, head_dim), BF16),
            pltpu.VMEM((heads_local, chips, rows_local, head_dim), BF16),
            pltpu.VMEM((2, all_rows), F32),
            pltpu.VMEM((head_dim, all_rows), F32),
            pltpu.VMEM((2,) + kv_own.shape, BF16),
            pltpu.VMEM((2,) + part_type.shape, BF16),
            pltpu.VMEM(dq_type.shape, BF16),
            pltpu.VMEM((1, rows), F32),
            pltpu.SemaphoreType.DMA((9 + 2 * heads_local + chips,)),
        ],
        compiler_params=alone,
        cost_estimate=pl.CostEstimate(
            flops=60 * all_rows * head_dim * (prefix + rows_local), bytes_accessed=8 * 2**20, transcendentals=0
        ),
    )(
        place, gathered, prefix_keys, prefix_values, span_keys, span_values, kv_par,
        positions.reshape(n_ctx, rows_local),
    )
    arrived = lax.all_to_all(dq, "ctx", 0, 0, axis_index_groups=same_core, tiled=True)
    returned = lax.ppermute(part_par, "ctx", swap)
    block = jax.ShapeDtypeStruct(part_type.shape[1:], BF16)
    ready = pl.pallas_call(
        add_kernel,
        out_shape=(block,) * n_head,
        in_specs=[smem, vmem, vmem],
        out_specs=(vmem,) * n_head,
        compiler_params=params,
    )(lax.axis_index("head").astype(jnp.int32).reshape(1), part_own, returned)
    terms = [ready[0]]
    for hop, sent in zip(hops(n_head)[1:], ready[1:]):
        terms.append(lax.ppermute(sent, "head", [(i, (i + hop) % n_head) for i in range(n_head)]))
    prefix_type = jax.ShapeDtypeStruct((prefix // n_head, head_dim), F32)
    span_type = jax.ShapeDtypeStruct((rows_local // n_head, head_dim), F32)
    return pl.pallas_call(
        sum_kernel,
        out_shape=(jax.ShapeDtypeStruct(queries.shape, F32), prefix_type, prefix_type, span_type, span_type),
        in_specs=[vmem] * (1 + n_head),
        out_specs=(vmem,) * 5,
        compiler_params=params,
    )(arrived, *terms)


def solution(mesh):
    in_specs = (
        P("ctx", "head"),
        P("ctx", "head"),
        P("ctx", "head"),
        P("head", "ctx"),
        P("ctx", None),
        P("ctx", None),
        P("ctx", None),
        P("ctx", None),
        P(),
        P("ctx"),
    )
    out_specs = (
        P("ctx", "head"),
        P(("ctx", "head"), None),
        P(("ctx", "head"), None),
        P(("ctx", "head"), None),
        P(("ctx", "head"), None),
    )
    body = functools.partial(shards, mesh.shape["ctx"], mesh.shape["head"])
    return jax.shard_map(body, mesh=mesh, in_specs=in_specs, out_specs=out_specs, check_vma=False)
```
